32 devices in a mesh: row: 4 (over y, core), col: 8 (over z, x).
Axes of the slice: x: 2, y: 2, z: 4, core: 2. Of those that a mesh axis runs over, the one named last changes fastest.
Arguments:
- fronts: bfloat16 [8, 1024, 1024], P('col', 'row')
- pivots: int32 [8], replicated, may hold values from 1 to 3, as said below
- targets: int32 [8, 4], replicated, may hold values from 0 to 7, as said below
- ancestor: bfloat16 [2, 1024, 2048], P(None, 'row', 'col'), may hold values from -1.5 to 1.5
Outputs:
- factor: float32 [8, 1024, 768], P('col', 'row')
- assembled: float32 [2, 1024, 2048], P(None, 'row', 'col')
The draws below stay inside these ranges and needn't reach their ends.
Inputs may be any that keep to these rules, and one draw needn't show every extreme that they name: `pivots`: every sibling eliminates at least one pivot block column; counts of 1 and of 3 both occur. targets[s, j] is j or j + 4; both ends of the range occur.
All inputs are finite; a program needn't handle non-finite values.
Results may differ from the reference program's by a relative error of at most 0.0011.
Values may be sent and summed in bfloat16 or wider, within the bound.
A program may use at most 128 MiB of HBM per device.

```python
import jax
import jax.numpy as jnp
from jax import lax

BLOCK = 256
STEPS = 3
FRONT_BLOCKS = 4
FRONT = 1024
ANCESTOR = 2048
SIBLINGS = 8


def draw_fronts(key, part):
    key = jax.random.fold_in(key, 11)
    width = BLOCK * FRONT_BLOCKS
    inner = width // 4

    def single(sibling):
        sub_key = jax.random.fold_in(key, sibling)
        factor_key, diag_key = jax.random.split(sub_key, 2)
        factor_draw = jax.random.normal(factor_key, (width, inner), jnp.float32)
        gram = jnp.dot(factor_draw, factor_draw.T, precision=lax.Precision.HIGHEST) / inner
        gram = 0.5 * (gram + gram.T)
        diagonal = jax.random.uniform(diag_key, (width,), jnp.float32, 0.25, 0.75)
        identity = jnp.arange(width)[:, None] == jnp.arange(width)[None, :]
        matrix = gram + jnp.where(identity, diagonal[:, None], 0.0)
        return matrix
    return lax.map(single, jnp.arange(SIBLINGS, dtype=jnp.int32)).astype(jnp.bfloat16)


def draw_pivots(key, part):
    key = jax.random.fold_in(key, 12)
    value_key, place_key, other_key = jax.random.split(key, 3)
    values = jax.random.randint(value_key, (SIBLINGS,), 1, STEPS + 1)
    place = jax.random.randint(place_key, (), 0, SIBLINGS)
    other = (place + 1 + jax.random.randint(other_key, (), 0, SIBLINGS - 1)) % SIBLINGS
    sibling_ids = jnp.arange(SIBLINGS, dtype=jnp.int32)
    values = jnp.where(sibling_ids == place, STEPS, jnp.where(sibling_ids == other, 1, values))
    return values.astype(jnp.int32)


def draw_targets(key, part):
    key = jax.random.fold_in(key, 13)
    bit_key, high_key, zero_key = jax.random.split(key, 3)
    halves = jax.random.randint(bit_key, (SIBLINGS, FRONT_BLOCKS), 0, 2)
    high_row = jax.random.randint(high_key, (), 0, SIBLINGS)
    zero_row = jax.random.randint(zero_key, (), 0, SIBLINGS)
    sibling_ids = jnp.arange(SIBLINGS, dtype=jnp.int32)[:, None]
    block_ids = jnp.arange(FRONT_BLOCKS, dtype=jnp.int32)[None, :]
    halves = jnp.where((sibling_ids == high_row) & (block_ids == FRONT_BLOCKS - 1), 1, halves)
    halves = jnp.where((sibling_ids == zero_row) & (block_ids == 0), 0, halves)
    return (block_ids + FRONT_BLOCKS * halves).astype(jnp.int32)


def block_scale(rng, dims, cuts, low, top_value):
    def one(dim, blocks):
        heights = jax.random.uniform(jax.random.fold_in(jax.random.fold_in(rng, 6), dim), (blocks,), jnp.float32, low / len(cuts), top_value / len(cuts))
        return jnp.repeat(jnp.exp(heights), dims[dim] // blocks).reshape((-1,) + (1,) * (len(dims) - dim - 1))

    gain = one(*cuts[0])
    for cut in cuts[1:]:
        gain = gain * one(*cut)
    return gain


def centred(stream_key, dims, spread, limit, cuts=(), kind=jnp.bfloat16):
    factor_of = block_scale(stream_key, dims, cuts, -0.22, 0.18) if cuts else 1.0
    array = jax.random.normal(stream_key, dims, jnp.float32) * spread * factor_of
    return jnp.minimum(jnp.maximum(array, -limit), limit).astype(kind)


def setup_inputs(seed: int = 0) -> dict:
    key_of = jax.random.split(jax.random.key(seed), 5)
    return {
        "fronts": draw_fronts(jax.random.fold_in(key_of[4], 71), 0),
        "pivots": draw_pivots(jax.random.fold_in(key_of[4], 71), 0),
        "targets": draw_targets(jax.random.fold_in(key_of[4], 71), 0),
        "ancestor": centred(key_of[3], (2, FRONT, ANCESTOR), 0.1, 1.5, ((1, 4), (2, 8))),
    }


def reference(fronts, pivots, targets, ancestor):
    width = BLOCK * FRONT_BLOCKS
    block_row = (jnp.arange(width, dtype=jnp.int32) // BLOCK).astype(jnp.int32)
    within = (jnp.arange(width, dtype=jnp.int32) % BLOCK).astype(jnp.int32)
    initial = ancestor.astype(jnp.float32).reshape(2 * width, 2 * width)

    def sibling_step(carried, inputs):
        front, pivot_count, target_row = inputs
        working = front.astype(jnp.float32)
        columns = []
        for section in range(STEPS):
            lower_edge = section * BLOCK
            upper_edge = lower_edge + BLOCK
            lower_block = jnp.linalg.cholesky(working[lower_edge:upper_edge, lower_edge:upper_edge])
            solved = jax.scipy.linalg.solve_triangular(lower_block, working[:, lower_edge:upper_edge].T, lower=True).T
            is_active = section < pivot_count
            own_block = jnp.where(block_row[:, None] > section, solved, jnp.zeros_like(solved))
            own_block = own_block.at[lower_edge:upper_edge].set(lower_block)
            columns.append(jnp.where(is_active, own_block, jnp.zeros_like(own_block)))
            outgoing = jnp.where(is_active & (block_row[:, None] > section), solved, jnp.zeros_like(solved)).astype(jnp.bfloat16)
            working = working - jnp.dot(outgoing.astype(jnp.float32), outgoing.T.astype(jnp.float32), preferred_element_type=jnp.float32)
        keep = block_row >= pivot_count
        contribution = jnp.where(keep[:, None] & keep[None, :], working, jnp.zeros_like(working))
        placed = (target_row[block_row] * BLOCK + within).astype(jnp.int32)
        carried = carried.at[placed[:, None], placed[None, :]].add(contribution)
        return (carried, jnp.concatenate(columns, axis=1))
    assembled, factor = lax.scan(sibling_step, initial, (fronts, pivots, targets))
    return (factor, assembled.reshape(2, width, 2 * width))
```

```python
import functools

import jax
import jax.numpy as jnp
from jax import lax
from jax.experimental import pallas as pl
from jax.experimental.pallas import tpu as pltpu
from jax.sharding import PartitionSpec as P

STEPS = 3
BASE = 128
GROUP = 8
F32 = jnp.float32
BF16 = jnp.bfloat16


def split(x):
    high = x.astype(BF16)
    return high, (x - high.astype(F32)).astype(BF16)


def dot3(a, b, dims):
    a_high, a_low = split(a)
    b_high, b_low = split(b)

    def one(x, y):
        return lax.dot_general(x, y, (dims, ((), ())), preferred_element_type=F32)

    return one(a_high, b_high) + (one(a_high, b_low) + one(a_low, b_high))


def splat(x, i, j):
    return jnp.broadcast_to(x[i : i + 1, j : j + 1], (GROUP, BASE))


def row_of(x, i):
    return jnp.broadcast_to(x[i : i + 1, :], (GROUP, BASE))


def column_of(x, j):
    return jnp.broadcast_to(x[:, j : j + 1], (GROUP, BASE))


def factor_base(matrix):
    count = BASE // GROUP
    sub = lax.broadcasted_iota(jnp.int32, (GROUP, BASE), 0)
    lane = lax.broadcasted_iota(jnp.int32, (GROUP, BASE), 1)
    left = [matrix[m * GROUP : (m + 1) * GROUP, :] for m in range(count)]
    right = [(lane == sub + m * GROUP).astype(F32) for m in range(count)]
    upper, inverse = [], []
    for g in range(count):
        first = g * GROUP
        s = {
            (i, j): splat(left[g], i, first + j)
            for i in range(GROUP)
            for j in range(i, GROUP)
        }
        rows = [row_of(left[g], i) for i in range(GROUP)]
        extra = [row_of(right[g], i) for i in range(GROUP)]
        scale, u = [], {}
        for i in range(GROUP):
            r = lax.rsqrt(s[i, i])
            scale.append(r)
            for j in range(i + 1, GROUP):
                u[i, j] = s[i, j] * r
            rows[i] = rows[i] * r
            extra[i] = extra[i] * r
            for j in range(i + 1, GROUP):
                for k in range(j, GROUP):
                    s[j, k] = s[j, k] - u[i, j] * u[i, k]
                rows[j] = rows[j] - u[i, j] * rows[i]
                extra[j] = extra[j] - u[i, j] * extra[i]
        top, bottom = rows[0], extra[0]
        for i in range(1, GROUP):
            top = jnp.where(sub == i, rows[i], top)
            bottom = jnp.where(sub == i, extra[i], bottom)
        upper.append(jnp.where(lane >= sub + first, top, 0.0))
        inverse.append(bottom)
        if g + 1 == count:
            break
        m = g + 1
        left_sum, right_sum = left[m], right[m]
        columns = [column_of(left[m], first + i) for i in range(GROUP)]
        for i in range(GROUP):
            columns[i] = columns[i] * scale[i]
            for j in range(i + 1, GROUP):
                columns[j] = columns[j] - u[i, j] * columns[i]
            left_sum = left_sum - columns[i] * rows[i]
            right_sum = right_sum - columns[i] * extra[i]
        left[m], right[m] = left_sum, right_sum
        if g + 2 == count:
            continue
        back, back_extra = [None] * GROUP, [None] * GROUP
        for i in reversed(range(GROUP)):
            a, b = rows[i], extra[i]
            for k in range(i + 1, GROUP):
                a = a - u[i, k] * back[k]
                b = b - u[i, k] * back_extra[k]
            back[i], back_extra[i] = a * scale[i], b * scale[i]
        for m in range(g + 2, count):
            left_sum, right_sum = left[m], right[m]
            for i in range(GROUP):
                column = column_of(left[m], first + i)
                left_sum = left_sum - column * back[i]
                right_sum = right_sum - column * back_extra[i]
            left[m], right[m] = left_sum, right_sum
    return jnp.concatenate(upper, axis=0), jnp.concatenate(inverse, axis=0)


def front_kernel(pivots_ref, slabs_ref, own_ref, factor_ref, out_ref, work, u_ref, p_ref):
    block = own_ref.shape[0]
    width = own_ref.shape[1]
    own_first = STEPS * block
    chunk = min(width, 1024)
    row_index = lax.axis_index("row")
    pivot_count = pivots_ref[lax.axis_index("col")]
    own_columns = pl.ds(pl.multiple_of(row_index * block, block), block)

    def chunks(body):
        if width == chunk:
            body(0)
        else:
            pl.loop(0, width // chunk)(lambda c: body(pl.multiple_of(c * chunk, chunk)))

    def load(c):
        columns = pl.ds(c, chunk)
        work[:own_first, columns] = slabs_ref[:, columns].astype(F32)
        work[own_first:, columns] = own_ref[:, columns].astype(F32)

    chunks(load)
    tri_row = lax.broadcasted_iota(jnp.int32, (block, block), 0)
    tri_column = lax.broadcasted_iota(jnp.int32, (block, block), 1)

    @pl.loop(0, STEPS)
    def _(t):
        active = t < pivot_count
        for half in range(block // BASE):
            first = pl.multiple_of(t * block + half * BASE, BASE)
            local = half * BASE
            upper, inverse = factor_base(work[pl.ds(first, BASE), pl.ds(first, BASE)])

            def solve(c):
                columns = pl.ds(c, chunk)
                u_ref[pl.ds(local, BASE), columns] = dot3(
                    inverse, work[pl.ds(first, BASE), columns], ((1,), (0,))
                )

            chunks(solve)
            u_ref[pl.ds(local, BASE), pl.ds(first, BASE)] = upper
            rest = block - local - BASE
            if rest:
                below = pl.multiple_of(first + BASE, BASE)
                left = u_ref[pl.ds(local, BASE), pl.ds(below, rest)]

                def update(c):
                    columns = pl.ds(c, chunk)
                    work[pl.ds(below, rest), columns] -= dot3(
                        left, u_ref[pl.ds(local, BASE), columns], ((0,), (0,))
                    )

                chunks(update)

        def round_panel(c):
            columns = pl.ds(c, chunk)
            place = lax.broadcasted_iota(jnp.int32, (block, chunk), 1) + c
            keep = (place >= (t + 1) * block) & active
            p_ref[:, columns] = jnp.where(keep, u_ref[:, columns], 0.0).astype(BF16)

        chunks(round_panel)
        own_factor = u_ref[:, own_columns].T
        keep = active & (row_index >= t) & ((row_index > t) | (tri_row >= tri_column))
        factor_ref[:, pl.ds(pl.multiple_of(t * block, block), block)] = jnp.where(
            keep, own_factor, 0.0
        )

        def trail(c):
            columns = pl.ds(c, chunk)
            right = p_ref[:, columns]
            for rows, left in (
                (pl.ds(block, own_first - block), p_ref[:, block:own_first]),
                (pl.ds(own_first, block), p_ref[:, own_columns]),
            ):
                work[rows, columns] -= lax.dot_general(
                    left, right, (((0,), (0,)), ((), ())), preferred_element_type=F32
                )

        chunks(trail)

    def store(c):
        columns = pl.ds(c, chunk)
        place = lax.broadcasted_iota(jnp.int32, (block, chunk), 1) + c
        keep = (place >= pivot_count * block) & (row_index >= pivot_count)
        out_ref[:, columns] = jnp.where(keep, work[own_first:, columns], 0.0)

    chunks(store)


def run_front(pivots, slabs, own):
    block, width = own.shape
    vmem = pl.BlockSpec(memory_space=pltpu.VMEM)
    return pl.pallas_call(
        front_kernel,
        out_shape=(
            jax.ShapeDtypeStruct((block, STEPS * block), F32),
            jax.ShapeDtypeStruct((block, width), F32),
        ),
        in_specs=[pl.BlockSpec(memory_space=pltpu.SMEM), vmem, vmem],
        out_specs=(vmem, vmem),
        scratch_shapes=[
            pltpu.VMEM(((STEPS + 1) * block, width), F32),
            pltpu.VMEM((block, width), F32),
            pltpu.VMEM((block, width), BF16),
        ],
        compiler_params=pltpu.CompilerParams(vmem_limit_bytes=56 * 1024 * 1024),
    )(pivots, slabs, own)


def shards(fronts, pivots, targets, ancestor):
    row_index = lax.axis_index("row")
    col_index = lax.axis_index("col")
    col_count = lax.axis_size("col")
    block_size = fronts.shape[1]
    width = fronts.shape[2]
    block_count = width // block_size
    gathered = lax.all_gather(fronts[0], "row", axis=0, tiled=True)
    factor, working = run_front(pivots, gathered[: STEPS * block_size], fronts[0])
    sibling_ids = jnp.arange(pivots.shape[0], dtype=jnp.int32)
    row_blocks = working.reshape(block_size, block_count, block_size)
    my_targets = jnp.sum(jnp.where(sibling_ids[:, None] == col_index, targets, 0), axis=0)
    dest_ids = jnp.arange(col_count, dtype=jnp.int32)
    owned_target = jnp.concatenate([my_targets, my_targets])
    keep = owned_target == dest_ids
    outgoing_blocks = jnp.where(
        keep[None, :, None], jnp.concatenate([row_blocks, row_blocks], axis=1), 0.0
    )
    received = lax.all_to_all(outgoing_blocks, "col", split_axis=1, concat_axis=1, tiled=True)
    block_ids = jnp.arange(block_count, dtype=jnp.int32)
    row_targets = jnp.sum(jnp.where(block_ids[None, :] == row_index, targets, 0), axis=1)
    halves = row_targets // block_count
    selector = (halves[None, :] == jnp.arange(2, dtype=jnp.int32)[:, None])[:, None, :, None]
    summed = jnp.sum(jnp.where(selector, received[None], 0.0), axis=2)
    return (factor[None], ancestor.astype(F32) + summed)


def solution(mesh):
    in_specs = (P("col", "row", None), P(), P(), P(None, "row", "col"))
    out_specs = (P("col", "row", None), P(None, "row", "col"))
    return jax.shard_map(shards, mesh=mesh, in_specs=in_specs, out_specs=out_specs, check_vma=False)
```

```python
import functools

import jax
import jax.numpy as jnp
from jax import lax
from jax.experimental import pallas as pl
from jax.experimental.pallas import tpu as pltpu
from jax.sharding import PartitionSpec as P

STEPS = 3
BASE = 128
GROUP = 8
MESH = pl.DeviceIdType.MESH
F32 = jnp.float32
BF16 = jnp.bfloat16


def split(x):
    high = x.astype(BF16)
    return high, (x - high.astype(F32)).astype(BF16)


def dot3(a, b, dims):
    a_high, a_low = split(a)
    b_high, b_low = split(b)

    def one(x, y):
        return lax.dot_general(x, y, (dims, ((), ())), preferred_element_type=F32)

    return one(a_high, b_high) + (one(a_high, b_low) + one(a_low, b_high))


def splat(x, i, j):
    return jnp.broadcast_to(x[i : i + 1, j : j + 1], (GROUP, BASE))


def row_of(x, i):
    return jnp.broadcast_to(x[i : i + 1, :], (GROUP, BASE))


def column_of(x, j):
    return jnp.broadcast_to(x[:, j : j + 1], (GROUP, BASE))


def factor_base(matrix):
    count = BASE // GROUP
    sub = lax.broadcasted_iota(jnp.int32, (GROUP, BASE), 0)
    lane = lax.broadcasted_iota(jnp.int32, (GROUP, BASE), 1)
    left = [matrix[m * GROUP : (m + 1) * GROUP, :] for m in range(count)]
    right = [(lane == sub + m * GROUP).astype(F32) for m in range(count)]
    upper, inverse = [], []
    for g in range(count):
        first = g * GROUP
        s = {
            (i, j): splat(left[g], i, first + j)
            for i in range(GROUP)
            for j in range(i, GROUP)
        }
        rows = [row_of(left[g], i) for i in range(GROUP)]
        extra = [row_of(right[g], i) for i in range(GROUP)]
        scale, u = [], {}
        for i in range(GROUP):
            r = lax.rsqrt(s[i, i])
            scale.append(r)
            for j in range(i + 1, GROUP):
                u[i, j] = s[i, j] * r
            rows[i] = rows[i] * r
            extra[i] = extra[i] * r
            for j in range(i + 1, GROUP):
                for k in range(j, GROUP):
                    s[j, k] = s[j, k] - u[i, j] * u[i, k]
                rows[j] = rows[j] - u[i, j] * rows[i]
                extra[j] = extra[j] - u[i, j] * extra[i]
        top, bottom = rows[0], extra[0]
        for i in range(1, GROUP):
            top = jnp.where(sub == i, rows[i], top)
            bottom = jnp.where(sub == i, extra[i], bottom)
        upper.append(jnp.where(lane >= sub + first, top, 0.0))
        inverse.append(bottom)
        if g + 1 == count:
            break
        m = g + 1
        left_sum, right_sum = left[m], right[m]
        columns = [column_of(left[m], first + i) for i in range(GROUP)]
        for i in range(GROUP):
            columns[i] = columns[i] * scale[i]
            for j in range(i + 1, GROUP):
                columns[j] = columns[j] - u[i, j] * columns[i]
            left_sum = left_sum - columns[i] * rows[i]
            right_sum = right_sum - columns[i] * extra[i]
        left[m], right[m] = left_sum, right_sum
        if g + 2 == count:
            continue
        back, back_extra = [None] * GROUP, [None] * GROUP
        for i in reversed(range(GROUP)):
            a, b = rows[i], extra[i]
            for k in range(i + 1, GROUP):
                a = a - u[i, k] * back[k]
                b = b - u[i, k] * back_extra[k]
            back[i], back_extra[i] = a * scale[i], b * scale[i]
        far_left = jnp.concatenate(left[g + 2 :], axis=0)
        far_right = jnp.concatenate(right[g + 2 :], axis=0)
        left_sum, right_sum = far_left, far_right
        for i in range(GROUP):
            column = jnp.broadcast_to(far_left[:, first + i : first + i + 1], far_left.shape)
            left_sum = left_sum - column * back[i][:1]
            right_sum = right_sum - column * back_extra[i][:1]
        for m in range(g + 2, count):
            place = (m - g - 2) * GROUP
            left[m] = left_sum[place : place + GROUP]
            right[m] = right_sum[place : place + GROUP]
    return jnp.concatenate(upper, axis=0), jnp.concatenate(inverse, axis=0)


LEVELS = 32767.0
TINY = 1e-30


def fused_kernel(
    rows,
    cols,
    pivots_ref,
    targets_ref,
    own_ref,
    ancestor_ref,
    factor_ref,
    out_ref,
    work,
    u_ref,
    p_ref,
    slabs,
    outgoing,
    out_scale,
    received,
    in_scale,
    row_send,
    row_recv,
    send_sem,
    scale_send,
    recv_sem,
    scale_recv,
):
    block = own_ref.shape[0]
    width = own_ref.shape[1]
    blocks = width // block
    own_first = STEPS * block
    chunk = min(width, 1024)
    row = lax.axis_index("row")
    col = lax.axis_index("col")
    core = lax.rem(row, 2)
    partner = row + 1 - 2 * core
    pivot_count = pivots_ref[col]
    own_columns = pl.ds(pl.multiple_of(row * block, block), block)

    barrier = pltpu.get_barrier_semaphore()
    for step in range(1, rows):
        pl.semaphore_signal(
            barrier, inc=1, device_id={"row": lax.rem(row + step, rows)}, device_id_type=MESH
        )
    for step in range(1, cols):
        pl.semaphore_signal(
            barrier, inc=1, device_id={"col": lax.rem(col + step, cols)}, device_id_type=MESH
        )
    pl.semaphore_wait(barrier, rows + cols - 2)

    pieces = [(0, 0, block), (0, block, width - block)]
    pieces += [(t, t * block, width - t * block) for t in range(1, STEPS)]

    def piece_copy(piece, source, target, slot):
        t, first, size = pieces[piece]
        columns = pl.ds(first, size)
        return pltpu.make_async_remote_copy(
            src_ref=source.at[:, columns] if source is own_ref else source.at[t, :, columns],
            dst_ref=slabs.at[t, :, columns],
            send_sem=row_send.at[piece, slot],
            recv_sem=row_recv.at[piece],
            device_id={"row": target},
            device_id_type=MESH,
        )

    def owner_copies(piece):
        slot = 0
        t = pieces[piece][0]
        copies = []
        for y in range(rows // 2):
            target = 2 * y + t % 2
            if target != t:
                copies.append(piece_copy(piece, own_ref, target, slot))
                slot += 1
        copies.append(piece_copy(piece, own_ref, t + 1 - 2 * (t % 2), slot))
        return copies

    def send_piece(piece):
        @pl.when(row == pieces[piece][0])
        def _():
            for copy in owner_copies(piece):
                copy.start()

    def arrive(piece):
        t, first, size = pieces[piece]

        @pl.when(row != t)
        def _():
            piece_copy(piece, slabs, partner, 0).wait_recv()

            @pl.when(core == t % 2)
            def _():
                piece_copy(piece, slabs, partner, 0).start()

            work[pl.ds(t * block, block), pl.ds(first, size)] = slabs[
                t, :, pl.ds(first, size)
            ].astype(F32)

        @pl.when(row == t)
        def _():
            work[pl.ds(t * block, block), pl.ds(first, size)] = own_ref[
                :, pl.ds(first, size)
            ].astype(F32)

    def chunks(body):
        if width == chunk:
            body(0)
        else:
            pl.loop(0, width // chunk)(lambda c: body(pl.multiple_of(c * chunk, chunk)))

    def block_copies(j, upper):
        target = j + upper * blocks
        return [
            pltpu.make_async_remote_copy(
                src_ref=source.at[j],
                dst_ref=sink.at[col],
                send_sem=sends.at[j, upper],
                recv_sem=recvs.at[col],
                device_id={"col": target},
                device_id_type=MESH,
            )
            for source, sink, sends, recvs in (
                (outgoing, received, send_sem, recv_sem),
                (out_scale, in_scale, scale_send, scale_recv),
            )
        ]

    def send_block(j):
        x = work[own_first:, j * block : (j + 1) * block]
        top = jnp.maximum(jnp.max(jnp.abs(x), axis=0, keepdims=True), TINY)
        outgoing[j] = jnp.floor(x * (LEVELS / top) + 0.5).astype(jnp.int32).astype(jnp.int16)
        out_scale[j] = jnp.broadcast_to(top * (1.0 / LEVELS), (GROUP, block))
        for upper in (1, 0):

            @pl.when(col != j + upper * blocks)
            def _():
                for copy in block_copies(j, upper):
                    copy.start()

            @pl.when(col == j + upper * blocks)
            def _():
                received[col] = outgoing[j]
                in_scale[col] = out_scale[j]

    send_piece(0)
    send_piece(1)
    work[own_first:, :] = own_ref[...].astype(F32)
    for t in range(1, STEPS):
        work[t * block : (t + 1) * block, : t * block] = jnp.zeros((block, t * block), F32)
    arrive(0)
    for piece in range(2, len(pieces)):
        send_piece(piece)
    tri_row = lax.broadcasted_iota(jnp.int32, (block, block), 0)
    tri_column = lax.broadcasted_iota(jnp.int32, (block, block), 1)

    @pl.loop(0, STEPS)
    def _(t):
        active = t < pivot_count

        @pl.loop(0, block // BASE)
        def _(half):
            local = pl.multiple_of(half * BASE, BASE)
            first = pl.multiple_of(t * block + local, BASE)
            upper, inverse = factor_base(work[pl.ds(first, BASE), pl.ds(first, BASE)])

            @pl.when((t == 0) & (half == 0))
            def _():
                arrive(1)

            def solve(c):
                columns = pl.ds(c, chunk)
                u_ref[pl.ds(local, BASE), columns] = dot3(
                    inverse, work[pl.ds(first, BASE), columns], ((1,), (0,))
                )

            chunks(solve)
            u_ref[pl.ds(local, BASE), pl.ds(first, BASE)] = upper

            @pl.when(half == 0)
            def _():
                below = pl.multiple_of(first + BASE, BASE)
                left = u_ref[pl.ds(local, BASE), pl.ds(below, BASE)]

                def update(c):
                    columns = pl.ds(c, chunk)
                    work[pl.ds(below, BASE), columns] -= dot3(
                        left, u_ref[pl.ds(local, BASE), columns], ((0,), (0,))
                    )

                chunks(update)

        def round_panel(c):
            columns = pl.ds(c, chunk)
            place = lax.broadcasted_iota(jnp.int32, (block, chunk), 1) + c
            keep = (place >= (t + 1) * block) & active
            p_ref[:, columns] = jnp.where(keep, u_ref[:, columns], 0.0).astype(BF16)

        chunks(round_panel)

        @pl.when(t == 0)
        def _():
            for piece in range(2, len(pieces)):
                arrive(piece)

        def trail(c):
            columns = pl.ds(c, chunk)
            right = p_ref[:, columns]
            for place, left in (
                (pl.ds(own_first, block), p_ref[:, own_columns]),
                (pl.ds(block, own_first - block), p_ref[:, block:own_first]),
            ):
                work[place, columns] -= lax.dot_general(
                    left, right, (((0,), (0,)), ((), ())), preferred_element_type=F32
                )

        chunks(trail)
        for j in range(1, blocks):
            level = jnp.minimum(row, min(j, STEPS))

            @pl.when(level == t + 1)
            def _():
                send_block(j)

        own_factor = u_ref[:, own_columns].T
        keep = active & (row >= t) & ((row > t) | (tri_row >= tri_column))
        factor_ref[:, pl.ds(pl.multiple_of(t * block, block), block)] = jnp.where(
            keep, own_factor, 0.0
        )

    out_ref[...] = ancestor_ref[...].astype(F32)
    mine = lax.rem(col, blocks)

    @pl.when((row >= 1) & (mine >= 1))
    def _():
        @pl.loop(0, cols)
        def _(source):
            @pl.when(source != col)
            def _():
                for sink, recvs in ((received, recv_sem), (in_scale, scale_recv)):
                    pltpu.make_async_remote_copy(
                        src_ref=sink.at[source],
                        dst_ref=sink.at[source],
                        send_sem=recvs.at[source],
                        recv_sem=recvs.at[source],
                        device_id={"col": source},
                        device_id_type=MESH,
                    ).wait_recv()

            values = received[source].astype(jnp.int32).astype(F32)
            scale = in_scale[source, 0:1, :]
            used = (pivots_ref[source] <= jnp.minimum(row, mine)) & (
                targets_ref[source, mine] == col
            )
            high = targets_ref[source, row] >= blocks
            out_ref[0] += values * jnp.where(used & ~high, scale, 0.0)
            out_ref[1] += values * jnp.where(used & high, scale, 0.0)

    for piece in range(len(pieces)):
        t = pieces[piece][0]

        @pl.when(row == t)
        def _():
            for copy in owner_copies(piece):
                copy.wait_send()

        @pl.when((row != t) & (core == t % 2))
        def _():
            piece_copy(piece, slabs, partner, 0).wait_send()

    @pl.when(row >= 1)
    def _():
        for j in range(1, blocks):
            for upper in (1, 0):

                @pl.when(col != j + upper * blocks)
                def _():
                    for copy in block_copies(j, upper):
                        copy.wait_send()


def shards(rows, cols, fronts, pivots, targets, ancestor):
    block, width = fronts.shape[1:]
    blocks = width // block
    vmem = pl.BlockSpec(memory_space=pltpu.VMEM)
    smem = pl.BlockSpec(memory_space=pltpu.SMEM)
    dma = pltpu.SemaphoreType.DMA
    factor, assembled = pl.pallas_call(
        functools.partial(fused_kernel, rows, cols),
        out_shape=(
            jax.ShapeDtypeStruct((block, STEPS * block), F32),
            jax.ShapeDtypeStruct(ancestor.shape, F32),
        ),
        in_specs=[smem, smem, vmem, vmem],
        out_specs=(vmem, vmem),
        scratch_shapes=[
            pltpu.VMEM(((STEPS + 1) * block, width), F32),
            pltpu.VMEM((block, width), F32),
            pltpu.VMEM((block, width), BF16),
            pltpu.VMEM((STEPS, block, width), BF16),
            pltpu.VMEM((blocks, block, block), jnp.int16),
            pltpu.VMEM((blocks, GROUP, block), F32),
            pltpu.VMEM((cols, block, block), jnp.int16),
            pltpu.VMEM((cols, GROUP, block), F32),
            dma((STEPS + 1, rows // 2)),
            dma((STEPS + 1,)),
            dma((blocks, 2)),
            dma((blocks, 2)),
            dma((cols,)),
            dma((cols,)),
        ],
        compiler_params=pltpu.CompilerParams(
            collective_id=0, has_side_effects=True, vmem_limit_bytes=56 * 1024 * 1024
        ),
    )(pivots, targets, fronts[0], ancestor)
    return (factor[None], assembled)


def solution(mesh):
    in_specs = (P("col", "row", None), P(), P(), P(None, "row", "col"))
    out_specs = (P("col", "row", None), P(None, "row", "col"))
    body = functools.partial(shards, mesh.shape["row"], mesh.shape["col"])
    return jax.shard_map(body, mesh=mesh, in_specs=in_specs, out_specs=out_specs, check_vma=False)
```

```python
import functools

import jax
import jax.numpy as jnp
from jax import lax
from jax.experimental import pallas as pl
from jax.experimental.pallas import tpu as pltpu
from jax.sharding import PartitionSpec as P

STEPS = 3
BASE = 128
GROUP = 8
MESH = pl.DeviceIdType.MESH
F32 = jnp.float32
BF16 = jnp.bfloat16


def split(x):
    high = x.astype(BF16)
    return high, (x - high.astype(F32)).astype(BF16)


def dot3(a, b, dims):
    a_high, a_low = split(a)
    b_high, b_low = split(b)

    def one(x, y):
        return lax.dot_general(x, y, (dims, ((), ())), preferred_element_type=F32)

    return one(a_high, b_high) + (one(a_high, b_low) + one(a_low, b_high))


def splat(x, i, j):
    return jnp.broadcast_to(x[i : i + 1, j : j + 1], (GROUP, BASE))


def row_of(x, i):
    return jnp.broadcast_to(x[i : i + 1, :], (GROUP, BASE))


def column_of(x, j):
    return jnp.broadcast_to(x[:, j : j + 1], (GROUP, BASE))


def factor_base(matrix):
    count = BASE // GROUP
    sub = lax.broadcasted_iota(jnp.int32, (GROUP, BASE), 0)
    lane = lax.broadcasted_iota(jnp.int32, (GROUP, BASE), 1)
    left = [matrix[m * GROUP : (m + 1) * GROUP, :] for m in range(count)]
    right = [(lane == sub + m * GROUP).astype(F32) for m in range(count)]
    upper, inverse = [], []
    for g in range(count):
        first = g * GROUP
        s = {
            (i, j): splat(left[g], i, first + j)
            for i in range(GROUP)
            for j in range(i, GROUP)
        }
        rows = [row_of(left[g], i) for i in range(GROUP)]
        extra = [row_of(right[g], i) for i in range(GROUP)]
        scale, u = [], {}
        for i in range(GROUP):
            r = lax.rsqrt(s[i, i])
            scale.append(r)
            for j in range(i + 1, GROUP):
                u[i, j] = s[i, j] * r
            rows[i] = rows[i] * r
            extra[i] = extra[i] * r
            for j in range(i + 1, GROUP):
                for k in range(j, GROUP):
                    s[j, k] = s[j, k] - u[i, j] * u[i, k]
                rows[j] = rows[j] - u[i, j] * rows[i]
                extra[j] = extra[j] - u[i, j] * extra[i]
        top, bottom = rows[0], extra[0]
        for i in range(1, GROUP):
            top = jnp.where(sub == i, rows[i], top)
            bottom = jnp.where(sub == i, extra[i], bottom)
        upper.append(jnp.where(lane >= sub + first, top, 0.0))
        inverse.append(bottom)
        if g + 1 == count:
            break
        m = g + 1
        left_sum, right_sum = left[m], right[m]
        columns = [column_of(left[m], first + i) for i in range(GROUP)]
        for i in range(GROUP):
            columns[i] = columns[i] * scale[i]
            for j in range(i + 1, GROUP):
                columns[j] = columns[j] - u[i, j] * columns[i]
            left_sum = left_sum - columns[i] * rows[i]
            right_sum = right_sum - columns[i] * extra[i]
        left[m], right[m] = left_sum, right_sum
        if g + 2 == count:
            continue
        back, back_extra = [None] * GROUP, [None] * GROUP
        for i in reversed(range(GROUP)):
            a, b = rows[i], extra[i]
            for k in range(i + 1, GROUP):
                a = a - u[i, k] * back[k]
                b = b - u[i, k] * back_extra[k]
            back[i], back_extra[i] = a * scale[i], b * scale[i]
        far_left = jnp.concatenate(left[g + 2 :], axis=0)
        far_right = jnp.concatenate(right[g + 2 :], axis=0)
        left_sum, right_sum = far_left, far_right
        for i in range(GROUP):
            column = jnp.broadcast_to(far_left[:, first + i : first + i + 1], far_left.shape)
            left_sum = left_sum - column * back[i][:1]
            right_sum = right_sum - column * back_extra[i][:1]
        for m in range(g + 2, count):
            place = (m - g - 2) * GROUP
            left[m] = left_sum[place : place + GROUP]
            right[m] = right_sum[place : place + GROUP]
    return jnp.concatenate(upper, axis=0), jnp.concatenate(inverse, axis=0)


LEVELS = 32767.0
TINY = 1e-30


def fused_kernel(
    rows,
    cols,
    pivots_ref,
    targets_ref,
    own_ref,
    factor_ref,
    out_ref,
    work,
    u_ref,
    p_ref,
    slabs,
    outgoing,
    out_scale,
    received,
    in_scale,
    row_send,
    row_recv,
    send_sem,
    scale_send,
    recv_sem,
    scale_recv,
):
    block = own_ref.shape[0]
    width = own_ref.shape[1]
    blocks = width // block
    own_first = STEPS * block
    chunk = min(width, 1024)
    row = lax.axis_index("row")
    col = lax.axis_index("col")
    core = lax.rem(row, 2)
    partner = row + 1 - 2 * core
    pivot_count = pivots_ref[col]
    own_columns = pl.ds(pl.multiple_of(row * block, block), block)

    barrier = pltpu.get_barrier_semaphore()
    for step in range(1, rows):
        pl.semaphore_signal(
            barrier, inc=1, device_id={"row": lax.rem(row + step, rows)}, device_id_type=MESH
        )
    for step in range(1, cols):
        pl.semaphore_signal(
            barrier, inc=1, device_id={"col": lax.rem(col + step, cols)}, device_id_type=MESH
        )
    pl.semaphore_wait(barrier, rows + cols - 2)

    pieces = [(0, 0, block), (0, block, width - block)]
    pieces += [(t, t * block, width - t * block) for t in range(1, STEPS)]

    def piece_copy(piece, source, target, slot):
        t, first, size = pieces[piece]
        columns = pl.ds(first, size)
        return pltpu.make_async_remote_copy(
            src_ref=source.at[:, columns] if source is own_ref else source.at[t, :, columns],
            dst_ref=slabs.at[t, :, columns],
            send_sem=row_send.at[piece, slot],
            recv_sem=row_recv.at[piece],
            device_id={"row": target},
            device_id_type=MESH,
        )

    def owner_copies(piece):
        slot = 0
        t = pieces[piece][0]
        copies = []
        for y in range(rows // 2):
            target = 2 * y + t % 2
            if target != t:
                copies.append(piece_copy(piece, own_ref, target, slot))
                slot += 1
        copies.append(piece_copy(piece, own_ref, t + 1 - 2 * (t % 2), slot))
        return copies

    def send_piece(piece):
        @pl.when(row == pieces[piece][0])
        def _():
            for copy in owner_copies(piece):
                copy.start()

    def arrive(piece):
        t, first, size = pieces[piece]

        @pl.when(row != t)
        def _():
            piece_copy(piece, slabs, partner, 0).wait_recv()

            @pl.when(core == t % 2)
            def _():
                piece_copy(piece, slabs, partner, 0).start()

            work[pl.ds(t * block, block), pl.ds(first, size)] = slabs[
                t, :, pl.ds(first, size)
            ].astype(F32)

        @pl.when(row == t)
        def _():
            work[pl.ds(t * block, block), pl.ds(first, size)] = own_ref[
                :, pl.ds(first, size)
            ].astype(F32)

    def chunks(body):
        if width == chunk:
            body(0)
        else:
            pl.loop(0, width // chunk)(lambda c: body(pl.multiple_of(c * chunk, chunk)))

    def block_copies(j, upper):
        target = j + upper * blocks
        return [
            pltpu.make_async_remote_copy(
                src_ref=source.at[j],
                dst_ref=sink.at[col],
                send_sem=sends.at[j, upper],
                recv_sem=recvs.at[col],
                device_id={"col": target},
                device_id_type=MESH,
            )
            for source, sink, sends, recvs in (
                (outgoing, received, send_sem, recv_sem),
                (out_scale, in_scale, scale_send, scale_recv),
            )
        ]

    def send_block(j):
        x = work[own_first:, j * block : (j + 1) * block]
        top = jnp.maximum(jnp.max(jnp.abs(x), axis=0, keepdims=True), TINY)
        outgoing[j] = jnp.floor(x * (LEVELS / top) + 0.5).astype(jnp.int32).astype(jnp.int16)
        out_scale[j] = jnp.broadcast_to(top * (1.0 / LEVELS), (GROUP, block))
        for upper in (1, 0):

            @pl.when(col != j + upper * blocks)
            def _():
                for copy in block_copies(j, upper):
                    copy.start()

            @pl.when(col == j + upper * blocks)
            def _():
                received[col] = outgoing[j]
                in_scale[col] = out_scale[j]

    def direct(source, t, height, first, size, target, index, slot):
        place = (pl.ds(0, height), pl.ds(first, size))
        return pltpu.make_async_remote_copy(
            src_ref=source.at[place],
            dst_ref=slabs.at[t, *place],
            send_sem=row_send.at[index, slot],
            recv_sem=row_recv.at[index],
            device_id={"row": target},
            device_id_type=MESH,
        )

    shares = [(0, BASE, 0, BASE), (0, block, BASE, block - BASE), (0, block, block, block)]
    shares += [(1, block, block, block)]

    def share(index, target):
        return direct(own_ref, *shares[index], target, index, target - 2)

    def take(index):
        t, height, first, size = shares[index]
        work[pl.ds(t * block, height), pl.ds(first, size)] = slabs[
            t, :height, pl.ds(first, size)
        ].astype(F32)

    def flip(source, t, j):
        x = source[:, t * block : (t + 1) * block].astype(F32)
        work[t * block : (t + 1) * block, j * block : (j + 1) * block] = x.T

    def flips(source, j):
        for t in range(2):
            flip(source, t, j)

    def partner_copy(r):
        if r == 0:
            return direct(own_ref, 0, block, 0, width, 1, 4, 0)
        size = width if r == 2 else 2 * block
        return direct(own_ref, 2, block, 0, size, 5 - r, 4, 0)

    def pair_start():
        @pl.when(row == 0)
        def _():
            for target in (2, 3):
                share(0, target).start()
            partner_copy(0).start()
            for index in (1, 2):
                for target in (2, 3):
                    share(index, target).start()

        for r in (2, 3):

            @pl.when(row == r)
            def _():
                partner_copy(r).start()

        work[own_first:, :] = own_ref[...].astype(F32)
        work[:own_first, :block] = jnp.zeros((own_first, block), F32)
        work[2 * block : own_first, : 2 * block] = jnp.zeros((block, 2 * block), F32)

        @pl.when(row == 0)
        def _():
            work[:block, :] = own_ref[...].astype(F32)

        @pl.when(row == 1)
        def _():
            partner_copy(0).wait_recv()
            for target in (2, 3):
                share(3, target).start()
            work[:block, :] = slabs[0].astype(F32)
            work[block : 2 * block, :] = own_ref[...].astype(F32)

        for r in (2, 3):

            @pl.when(row == r)
            def _():
                flips(own_ref, r)
                if r == 2:
                    work[2 * block : own_first, :] = own_ref[...].astype(F32)
                share(0, r).wait_recv()
                take(0)

    def pair_middle():
        for r in (2, 3):

            @pl.when(row == r)
            def _():
                partner_copy(5 - r).wait_recv()
                flips(slabs.at[2], 5 - r)
                if r == 3:
                    work[2 * block : own_first, :] = slabs[2].astype(F32)
                for index in (1, 2):
                    share(index, r).wait_recv()
                    take(index)

    def pair_late():
        for r in (2, 3):

            @pl.when(row == r)
            def _():
                share(3, r).wait_recv()
                take(3)

    def pair_finish():
        @pl.when(row == 0)
        def _():
            for target in (2, 3):
                for index in (0, 1, 2):
                    share(index, target).wait_send()
            partner_copy(0).wait_send()

        @pl.when(row == 1)
        def _():
            for target in (2, 3):
                share(3, target).wait_send()

        for r in (2, 3):

            @pl.when(row == r)
            def _():
                partner_copy(r).wait_send()

    def slab_start():
        send_piece(0)
        send_piece(1)
        work[own_first:, :] = own_ref[...].astype(F32)
        for t in range(1, STEPS):
            work[t * block : (t + 1) * block, : t * block] = jnp.zeros((block, t * block), F32)
        arrive(0)
        for piece in range(2, len(pieces)):
            send_piece(piece)

    def slab_middle():
        arrive(1)

    def slab_late():
        for piece in range(2, len(pieces)):
            arrive(piece)

    def slab_finish():
        for piece in range(len(pieces)):
            t = pieces[piece][0]

            @pl.when(row == t)
            def _():
                for copy in owner_copies(piece):
                    copy.wait_send()

            @pl.when((row != t) & (core == t % 2))
            def _():
                piece_copy(piece, slabs, partner, 0).wait_send()

    if rows == 4 and blocks == 4:
        start, middle, late, finish = pair_start, pair_middle, pair_late, pair_finish
    else:
        start, middle, late, finish = slab_start, slab_middle, slab_late, slab_finish
    start()
    tri_row = lax.broadcasted_iota(jnp.int32, (block, block), 0)
    tri_column = lax.broadcasted_iota(jnp.int32, (block, block), 1)
    factor_ref[:, block:] = jnp.zeros((block, (STEPS - 1) * block), F32)

    @pl.loop(0, jnp.minimum(row + 1, STEPS))
    def _(t):
        active = t < pivot_count

        @pl.loop(0, block // BASE)
        def _(half):
            local = pl.multiple_of(half * BASE, BASE)
            first = pl.multiple_of(t * block + local, BASE)
            upper, inverse = factor_base(work[pl.ds(first, BASE), pl.ds(first, BASE)])

            @pl.when((t == 0) & (half == 0))
            def _():
                middle()

            def solve(c):
                columns = pl.ds(c, chunk)
                u_ref[pl.ds(local, BASE), columns] = dot3(
                    inverse, work[pl.ds(first, BASE), columns], ((1,), (0,))
                )

            chunks(solve)
            u_ref[pl.ds(local, BASE), pl.ds(first, BASE)] = upper

            @pl.when(half == 0)
            def _():
                below = pl.multiple_of(first + BASE, BASE)
                left = u_ref[pl.ds(local, BASE), pl.ds(below, BASE)]

                def update(c):
                    columns = pl.ds(c, chunk)
                    work[pl.ds(below, BASE), columns] -= dot3(
                        left, u_ref[pl.ds(local, BASE), columns], ((0,), (0,))
                    )

                chunks(update)

        def round_panel(c):
            columns = pl.ds(c, chunk)
            place = lax.broadcasted_iota(jnp.int32, (block, chunk), 1) + c
            keep = (place >= (t + 1) * block) & active
            p_ref[:, columns] = jnp.where(keep, u_ref[:, columns], 0.0).astype(BF16)

        chunks(round_panel)

        @pl.when(t == 0)
        def _():
            late()

        def trail(c):
            columns = pl.ds(c, chunk)
            right = p_ref[:, columns]
            for place, left in (
                (pl.ds(own_first, block), p_ref[:, own_columns]),
                (pl.ds(block, own_first - block), p_ref[:, block:own_first]),
            ):
                work[place, columns] -= lax.dot_general(
                    left, right, (((0,), (0,)), ((), ())), preferred_element_type=F32
                )

        chunks(trail)
        for j in range(1, blocks):
            level = jnp.minimum(row, min(j, STEPS))

            @pl.when(level == t + 1)
            def _():
                send_block(j)

        keep = active & ((row > t) | (tri_row >= tri_column))
        factor_ref[:, pl.ds(pl.multiple_of(t * block, block), block)] = jnp.where(
            keep, -u_ref[:, own_columns].T, 0.0
        )

    out_ref[...] = jnp.zeros_like(out_ref)
    mine = lax.rem(col, blocks)

    @pl.when((row >= 1) & (mine >= 1))
    def _():
        @pl.loop(0, cols)
        def _(source):
            @pl.when(source != col)
            def _():
                for sink, recvs in ((received, recv_sem), (in_scale, scale_recv)):
                    pltpu.make_async_remote_copy(
                        src_ref=sink.at[source],
                        dst_ref=sink.at[source],
                        send_sem=recvs.at[source],
                        recv_sem=recvs.at[source],
                        device_id={"col": source},
                        device_id_type=MESH,
                    ).wait_recv()

            values = received[source].astype(jnp.int32).astype(F32)
            scale = in_scale[source, 0:1, :]
            used = (pivots_ref[source] <= jnp.minimum(row, mine)) & (
                targets_ref[mine, source] == col
            )
            high = targets_ref[row, source] >= blocks
            out_ref[0] += values * jnp.where(used & ~high, scale, 0.0)
            out_ref[1] += values * jnp.where(used & high, scale, 0.0)

    finish()

    @pl.when(row >= 1)
    def _():
        for j in range(1, blocks):
            for upper in (1, 0):

                @pl.when(col != j + upper * blocks)
                def _():
                    for copy in block_copies(j, upper):
                        copy.wait_send()


def shards(rows, cols, fronts, pivots, targets, ancestor):
    block, width = fronts.shape[1:]
    blocks = width // block
    vmem = pl.BlockSpec(memory_space=pltpu.VMEM)
    smem = pl.BlockSpec(memory_space=pltpu.SMEM)
    dma = pltpu.SemaphoreType.DMA
    negated, added = pl.pallas_call(
        functools.partial(fused_kernel, rows, cols),
        out_shape=(
            jax.ShapeDtypeStruct((block, STEPS * block), F32),
            jax.ShapeDtypeStruct(ancestor.shape, F32),
        ),
        in_specs=[smem, smem, vmem],
        out_specs=(vmem, vmem),
        scratch_shapes=[
            pltpu.VMEM(((STEPS + 1) * block, width), F32),
            pltpu.VMEM((block, width), F32),
            pltpu.VMEM((block, width), BF16),
            pltpu.VMEM((STEPS, block, width), BF16),
            pltpu.VMEM((blocks, block, block), jnp.int16),
            pltpu.VMEM((blocks, GROUP, block), F32),
            pltpu.VMEM((cols, block, block), jnp.int16),
            pltpu.VMEM((cols, GROUP, block), F32),
            dma((STEPS + 2, rows // 2)),
            dma((STEPS + 2,)),
            dma((blocks, 2)),
            dma((blocks, 2)),
            dma((cols,)),
            dma((cols,)),
        ],
        compiler_params=pltpu.CompilerParams(
            collective_id=0, has_side_effects=True, vmem_limit_bytes=56 * 1024 * 1024
        ),
    )(pivots, targets.T, fronts[0])
    return (-negated[None], ancestor.astype(F32) + added)


def solution(mesh):
    in_specs = (P("col", "row", None), P(), P(), P(None, "row", "col"))
    out_specs = (P("col", "row", None), P(None, "row", "col"))
    body = functools.partial(shards, mesh.shape["row"], mesh.shape["col"])
    return jax.shard_map(body, mesh=mesh, in_specs=in_specs, out_specs=out_specs, check_vma=False)
```

```python
import functools

import jax
import jax.numpy as jnp
from jax import lax
from jax.experimental import pallas as pl
from jax.experimental.pallas import tpu as pltpu
from jax.sharding import PartitionSpec as P

STEPS = 3
BASE = 128
GROUP = 8
MESH = pl.DeviceIdType.MESH
F32 = jnp.float32
BF16 = jnp.bfloat16


def split(x):
    high = x.astype(BF16)
    return high, (x - high.astype(F32)).astype(BF16)


def dot3(a, b, dims):
    a_high, a_low = split(a)
    b_high, b_low = split(b)

    def one(x, y):
        return lax.dot_general(x, y, (dims, ((), ())), preferred_element_type=F32)

    return one(a_high, b_high) + (one(a_high, b_low) + one(a_low, b_high))


def splat(x, i, j):
    return jnp.broadcast_to(x[i : i + 1, j : j + 1], (GROUP, BASE))


def row_of(x, i):
    return jnp.broadcast_to(x[i : i + 1, :], (GROUP, BASE))


def column_of(x, j):
    return jnp.broadcast_to(x[:, j : j + 1], (GROUP, BASE))


def factor_base(matrix):
    count = BASE // GROUP
    sub = lax.broadcasted_iota(jnp.int32, (GROUP, BASE), 0)
    lane = lax.broadcasted_iota(jnp.int32, (GROUP, BASE), 1)
    left = [matrix[m * GROUP : (m + 1) * GROUP, :] for m in range(count)]
    right = [(lane == sub + m * GROUP).astype(F32) for m in range(count)]
    spots = [jnp.where(right[m] > 0.0, left[m], 0.0) for m in range(count)]
    diagonal = jnp.sum(sum(spots), axis=0, keepdims=True)
    shrink = lax.rsqrt(diagonal)
    for m in range(count):
        tall = lax.rsqrt(jnp.sum(spots[m], axis=1, keepdims=True))
        left[m] = left[m] * tall * shrink
    upper, inverse = [], []
    for g in range(count):
        first = g * GROUP
        s = {
            (i, j): splat(left[g], i, first + j)
            for i in range(GROUP)
            for j in range(i, GROUP)
        }
        rows = [row_of(left[g], i) for i in range(GROUP)]
        extra = [row_of(right[g], i) for i in range(GROUP)]
        scale, u = [None] * GROUP, {}
        for p in range(0, GROUP, 2):
            q = p + 1
            a, b = s[p, p], s[p, q]
            r = lax.rsqrt(a)
            d = lax.rsqrt(a * s[q, q] - b * b)
            both = d * r
            scale[p], scale[q] = r, a * both
            u[p, q] = b * r
            for j in range(q + 1, GROUP):
                u[p, j] = s[p, j] * r
                u[q, j] = (a * s[q, j] - b * s[p, j]) * both
            for j in range(q + 1, GROUP):
                for k in range(j, GROUP):
                    s[j, k] = (s[j, k] - u[p, j] * u[p, k]) - u[q, j] * u[q, k]
            for x in (rows, extra):
                x[p] = x[p] * r
                x[q] = (x[q] - u[p, q] * x[p]) * scale[q]
                for j in range(q + 1, GROUP):
                    x[j] = (x[j] - u[p, j] * x[p]) - u[q, j] * x[q]
        top, bottom = rows[0], extra[0]
        for i in range(1, GROUP):
            top = jnp.where(sub == i, rows[i], top)
            bottom = jnp.where(sub == i, extra[i], bottom)
        upper.append(jnp.where(lane >= sub + first, top, 0.0))
        inverse.append(bottom)
        if g + 1 == count:
            break
        m = g + 1
        left_sum, right_sum = left[m], right[m]
        columns = [column_of(left[m], first + i) for i in range(GROUP)]
        for i in range(GROUP):
            columns[i] = columns[i] * scale[i]
            for j in range(i + 1, GROUP):
                columns[j] = columns[j] - u[i, j] * columns[i]
            left_sum = left_sum - columns[i] * rows[i]
            right_sum = right_sum - columns[i] * extra[i]
        left[m], right[m] = left_sum, right_sum
        if g + 2 == count:
            continue
        back, back_extra = [None] * GROUP, [None] * GROUP
        for i in reversed(range(GROUP)):
            a, b = rows[i], extra[i]
            for k in range(i + 1, GROUP):
                a = a - u[i, k] * back[k]
                b = b - u[i, k] * back_extra[k]
            back[i], back_extra[i] = a * scale[i], b * scale[i]
        far_left = jnp.stack(left[g + 2 :])
        left_sum, right_sum = far_left, jnp.stack(right[g + 2 :])
        for i in range(GROUP):
            column = jnp.broadcast_to(far_left[:, :, first + i : first + i + 1], far_left.shape)
            left_sum = left_sum - column * back[i][None]
            right_sum = right_sum - column * back_extra[i][None]
        for m in range(g + 2, count):
            left[m] = left_sum[m - g - 2]
            right[m] = right_sum[m - g - 2]
    upper = jnp.concatenate(upper, axis=0) * (diagonal * shrink)
    return upper, jnp.concatenate(inverse, axis=0) * shrink


LEVELS = 32767.0
TINY = 1e-30


def fused_kernel(
    rows,
    cols,
    pivots_ref,
    targets_ref,
    own_ref,
    factor_ref,
    out_ref,
    work,
    u_ref,
    p_ref,
    slabs,
    outgoing,
    out_scale,
    received,
    in_scale,
    row_send,
    row_recv,
    send_sem,
    scale_send,
    recv_sem,
    scale_recv,
):
    block = own_ref.shape[0]
    width = own_ref.shape[1]
    blocks = width // block
    own_first = STEPS * block
    chunk = min(width, 1024)
    row = lax.axis_index("row")
    col = lax.axis_index("col")
    core = lax.rem(row, 2)
    partner = row + 1 - 2 * core
    pivot_count = pivots_ref[col]
    own_columns = pl.ds(pl.multiple_of(row * block, block), block)

    barrier = pltpu.get_barrier_semaphore()
    for step in range(1, rows):
        pl.semaphore_signal(
            barrier, inc=1, device_id={"row": lax.rem(row + step, rows)}, device_id_type=MESH
        )
    for step in range(1, cols):
        pl.semaphore_signal(
            barrier, inc=1, device_id={"col": lax.rem(col + step, cols)}, device_id_type=MESH
        )
    pl.semaphore_wait(barrier, rows + cols - 2)

    pieces = [(0, 0, block), (0, block, width - block)]
    pieces += [(t, t * block, width - t * block) for t in range(1, STEPS)]

    def piece_copy(piece, source, target, slot):
        t, first, size = pieces[piece]
        columns = pl.ds(first, size)
        return pltpu.make_async_remote_copy(
            src_ref=source.at[:, columns] if source is own_ref else source.at[t, :, columns],
            dst_ref=slabs.at[t, :, columns],
            send_sem=row_send.at[piece, slot],
            recv_sem=row_recv.at[piece],
            device_id={"row": target},
            device_id_type=MESH,
        )

    def owner_copies(piece):
        slot = 0
        t = pieces[piece][0]
        copies = []
        for y in range(rows // 2):
            target = 2 * y + t % 2
            if target != t:
                copies.append(piece_copy(piece, own_ref, target, slot))
                slot += 1
        copies.append(piece_copy(piece, own_ref, t + 1 - 2 * (t % 2), slot))
        return copies

    def send_piece(piece):
        @pl.when(row == pieces[piece][0])
        def _():
            for copy in owner_copies(piece):
                copy.start()

    def arrive(piece):
        t, first, size = pieces[piece]

        @pl.when(row != t)
        def _():
            piece_copy(piece, slabs, partner, 0).wait_recv()

            @pl.when(core == t % 2)
            def _():
                piece_copy(piece, slabs, partner, 0).start()

            work[pl.ds(t * block, block), pl.ds(first, size)] = slabs[
                t, :, pl.ds(first, size)
            ].astype(F32)

        @pl.when(row == t)
        def _():
            work[pl.ds(t * block, block), pl.ds(first, size)] = own_ref[
                :, pl.ds(first, size)
            ].astype(F32)

    def chunks(body):
        if width == chunk:
            body(0)
        else:
            pl.loop(0, width // chunk)(lambda c: body(pl.multiple_of(c * chunk, chunk)))

    def block_copies(j, upper):
        target = j + upper * blocks
        return [
            pltpu.make_async_remote_copy(
                src_ref=source.at[j],
                dst_ref=sink.at[col],
                send_sem=sends.at[j, upper],
                recv_sem=recvs.at[col],
                device_id={"col": target},
                device_id_type=MESH,
            )
            for source, sink, sends, recvs in (
                (outgoing, received, send_sem, recv_sem),
                (out_scale, in_scale, scale_send, scale_recv),
            )
        ]

    def send_block(j):
        x = work[own_first:, j * block : (j + 1) * block]
        top = jnp.maximum(jnp.max(jnp.abs(x), axis=0, keepdims=True), TINY)
        outgoing[j] = jnp.floor(x * (LEVELS / top) + 0.5).astype(jnp.int32).astype(jnp.int16)
        out_scale[j] = jnp.broadcast_to(top * (1.0 / LEVELS), (GROUP, block))
        for upper in (1, 0):

            @pl.when(col != j + upper * blocks)
            def _():
                for copy in block_copies(j, upper):
                    copy.start()

            @pl.when(col == j + upper * blocks)
            def _():
                received[col] = outgoing[j]
                in_scale[col] = out_scale[j]

    def direct(source, t, height, first, size, target, index, slot):
        place = (pl.ds(0, height), pl.ds(first, size))
        return pltpu.make_async_remote_copy(
            src_ref=source.at[place],
            dst_ref=slabs.at[t, *place],
            send_sem=row_send.at[index, slot],
            recv_sem=row_recv.at[index],
            device_id={"row": target},
            device_id_type=MESH,
        )

    shares = [(0, BASE, 0, BASE), (0, block, BASE, block - BASE), (0, block, block, block)]
    shares += [(1, block, block, block)]

    def share(index, target):
        return direct(own_ref, *shares[index], target, index, target - 2)

    def take(index):
        t, height, first, size = shares[index]
        work[pl.ds(t * block, height), pl.ds(first, size)] = slabs[
            t, :height, pl.ds(first, size)
        ].astype(F32)

    def flip(source, t, j):
        x = source[:, t * block : (t + 1) * block].astype(F32)
        work[t * block : (t + 1) * block, j * block : (j + 1) * block] = x.T

    def flips(source, j):
        for t in range(2):
            flip(source, t, j)

    def partner_copy(r):
        if r == 0:
            return direct(own_ref, 0, block, 0, width, 1, 4, 0)
        size = width if r == 2 else 2 * block
        return direct(own_ref, 2, block, 0, size, 5 - r, 4, 0)

    def pair_start():
        @pl.when(row == 0)
        def _():
            for target in (2, 3):
                share(0, target).start()
            partner_copy(0).start()
            for index in (1, 2):
                for target in (2, 3):
                    share(index, target).start()

        for r in (2, 3):

            @pl.when(row == r)
            def _():
                partner_copy(r).start()

        work[own_first:, :] = own_ref[...].astype(F32)
        work[:own_first, :block] = jnp.zeros((own_first, block), F32)
        work[2 * block : own_first, : 2 * block] = jnp.zeros((block, 2 * block), F32)

        @pl.when(row == 0)
        def _():
            work[:block, :] = own_ref[...].astype(F32)

        @pl.when(row == 1)
        def _():
            partner_copy(0).wait_recv()
            for target in (2, 3):
                share(3, target).start()
            work[:block, :] = slabs[0].astype(F32)
            work[block : 2 * block, :] = own_ref[...].astype(F32)

        for r in (2, 3):

            @pl.when(row == r)
            def _():
                flips(own_ref, r)
                if r == 2:
                    work[2 * block : own_first, :] = own_ref[...].astype(F32)
                share(0, r).wait_recv()
                take(0)

    def pair_middle():
        for r in (2, 3):

            @pl.when(row == r)
            def _():
                partner_copy(5 - r).wait_recv()
                flips(slabs.at[2], 5 - r)
                if r == 3:
                    work[2 * block : own_first, :] = slabs[2].astype(F32)
                for index in (1, 2):
                    share(index, r).wait_recv()
                    take(index)

    def pair_late():
        for r in (2, 3):

            @pl.when(row == r)
            def _():
                share(3, r).wait_recv()
                take(3)

    def pair_finish():
        @pl.when(row == 0)
        def _():
            for target in (2, 3):
                for index in (0, 1, 2):
                    share(index, target).wait_send()
            partner_copy(0).wait_send()

        @pl.when(row == 1)
        def _():
            for target in (2, 3):
                share(3, target).wait_send()

        for r in (2, 3):

            @pl.when(row == r)
            def _():
                partner_copy(r).wait_send()

    def slab_start():
        send_piece(0)
        send_piece(1)
        work[own_first:, :] = own_ref[...].astype(F32)
        for t in range(1, STEPS):
            work[t * block : (t + 1) * block, : t * block] = jnp.zeros((block, t * block), F32)
        arrive(0)
        for piece in range(2, len(pieces)):
            send_piece(piece)

    def slab_middle():
        arrive(1)

    def slab_late():
        for piece in range(2, len(pieces)):
            arrive(piece)

    def slab_finish():
        for piece in range(len(pieces)):
            t = pieces[piece][0]

            @pl.when(row == t)
            def _():
                for copy in owner_copies(piece):
                    copy.wait_send()

            @pl.when((row != t) & (core == t % 2))
            def _():
                piece_copy(piece, slabs, partner, 0).wait_send()

    if rows == 4 and blocks == 4:
        start, middle, late, finish = pair_start, pair_middle, pair_late, pair_finish
    else:
        start, middle, late, finish = slab_start, slab_middle, slab_late, slab_finish
    start()
    tri_row = lax.broadcasted_iota(jnp.int32, (block, block), 0)
    tri_column = lax.broadcasted_iota(jnp.int32, (block, block), 1)
    factor_ref[:, block:] = jnp.zeros((block, (STEPS - 1) * block), F32)

    @pl.loop(0, jnp.minimum(row + 1, STEPS))
    def _(t):
        active = t < pivot_count

        top = pl.ds(pl.multiple_of(t * block, BASE), BASE)
        low = pl.ds(pl.multiple_of(t * block + BASE, BASE), BASE)
        upper, inverse = factor_base(work[top, top])

        @pl.when(t == 0)
        def _():
            middle()

        cross = dot3(inverse, work[top, low], ((1,), (0,)))
        low_upper, low_inverse = factor_base(work[low, low] - dot3(cross, cross, ((0,), (0,))))

        def solve(c):
            columns = pl.ds(c, chunk)
            solved = dot3(inverse, work[top, columns], ((1,), (0,)))
            u_ref[:BASE, columns] = solved
            work[low, columns] -= dot3(cross, solved, ((0,), (0,)))

        def solve_low(c):
            columns = pl.ds(c, chunk)
            u_ref[BASE:, columns] = dot3(low_inverse, work[low, columns], ((1,), (0,)))

        chunks(solve)
        chunks(solve_low)
        u_ref[:BASE, top] = upper
        u_ref[BASE:, low] = low_upper

        def round_panel(c):
            columns = pl.ds(c, chunk)
            place = lax.broadcasted_iota(jnp.int32, (block, chunk), 1) + c
            keep = (place >= (t + 1) * block) & active
            p_ref[:, columns] = jnp.where(keep, u_ref[:, columns], 0.0).astype(BF16)

        chunks(round_panel)

        @pl.when(t == 0)
        def _():
            late()

        keep = active & ((row > t) | (tri_row >= tri_column))
        factor_ref[:, pl.ds(pl.multiple_of(t * block, block), block)] = jnp.where(
            keep, -u_ref[:, own_columns].T, 0.0
        )

        def outer(left, columns):
            dims = (((0,), (0,)), ((), ()))
            return lax.dot_general(left, p_ref[:, columns], dims, preferred_element_type=F32)

        def trail(c):
            columns = pl.ds(c, chunk)
            work[pl.ds(own_first, block), columns] -= outer(p_ref[:, own_columns], columns)

            @pl.when(t + 1 < STEPS)
            def _():
                work[block:own_first, columns] -= outer(p_ref[:, block:own_first], columns)

        chunks(trail)
        for j in range(1, blocks):
            level = jnp.minimum(row, min(j, STEPS))

            @pl.when(level == t + 1)
            def _():
                send_block(j)

    out_ref[...] = jnp.zeros_like(out_ref)
    mine = lax.rem(col, blocks)

    @pl.when((row >= 1) & (mine >= 1))
    def _():
        @pl.loop(0, cols)
        def _(source):
            @pl.when(source != col)
            def _():
                for sink, recvs in ((received, recv_sem), (in_scale, scale_recv)):
                    pltpu.make_async_remote_copy(
                        src_ref=sink.at[source],
                        dst_ref=sink.at[source],
                        send_sem=recvs.at[source],
                        recv_sem=recvs.at[source],
                        device_id={"col": source},
                        device_id_type=MESH,
                    ).wait_recv()

            values = received[source].astype(jnp.int32).astype(F32)
            scale = in_scale[source, 0:1, :]
            used = (pivots_ref[source] <= jnp.minimum(row, mine)) & (
                targets_ref[mine, source] == col
            )
            high = targets_ref[row, source] >= blocks
            out_ref[0] += values * jnp.where(used & ~high, scale, 0.0)
            out_ref[1] += values * jnp.where(used & high, scale, 0.0)

    finish()

    @pl.when(row >= 1)
    def _():
        for j in range(1, blocks):
            for upper in (1, 0):

                @pl.when(col != j + upper * blocks)
                def _():
                    for copy in block_copies(j, upper):
                        copy.wait_send()


def shards(rows, cols, fronts, pivots, targets, ancestor):
    block, width = fronts.shape[1:]
    blocks = width // block
    vmem = pl.BlockSpec(memory_space=pltpu.VMEM)
    smem = pl.BlockSpec(memory_space=pltpu.SMEM)
    dma = pltpu.SemaphoreType.DMA
    negated, added = pl.pallas_call(
        functools.partial(fused_kernel, rows, cols),
        out_shape=(
            jax.ShapeDtypeStruct((block, STEPS * block), F32),
            jax.ShapeDtypeStruct(ancestor.shape, F32),
        ),
        in_specs=[smem, smem, vmem],
        out_specs=(vmem, vmem),
        scratch_shapes=[
            pltpu.VMEM(((STEPS + 1) * block, width), F32),
            pltpu.VMEM((block, width), F32),
            pltpu.VMEM((block, width), BF16),
            pltpu.VMEM((STEPS, block, width), BF16),
            pltpu.VMEM((blocks, block, block), jnp.int16),
            pltpu.VMEM((blocks, GROUP, block), F32),
            pltpu.VMEM((cols, block, block), jnp.int16),
            pltpu.VMEM((cols, GROUP, block), F32),
            dma((STEPS + 2, rows // 2)),
            dma((STEPS + 2,)),
            dma((blocks, 2)),
            dma((blocks, 2)),
            dma((cols,)),
            dma((cols,)),
        ],
        compiler_params=pltpu.CompilerParams(
            collective_id=0, has_side_effects=True, vmem_limit_bytes=56 * 1024 * 1024
        ),
    )(pivots, targets.T, fronts[0])
    return (-negated[None], ancestor.astype(F32) + added)


def solution(mesh):
    in_specs = (P("col", "row", None), P(), P(), P(None, "row", "col"))
    out_specs = (P("col", "row", None), P(None, "row", "col"))
    body = functools.partial(shards, mesh.shape["row"], mesh.shape["col"])
    return jax.shard_map(body, mesh=mesh, in_specs=in_specs, out_specs=out_specs, check_vma=False)
```

```python
import functools

import jax
import jax.numpy as jnp
from jax import lax
from jax.experimental import pallas as pl
from jax.experimental.pallas import tpu as pltpu
from jax.sharding import PartitionSpec as P

STEPS = 3
BASE = 128
GROUP = 8
MESH = pl.DeviceIdType.MESH
F32 = jnp.float32
BF16 = jnp.bfloat16


def split(x):
    high = x.astype(BF16)
    return high, (x - high.astype(F32)).astype(BF16)


def dot3(a, b, dims):
    a_high, a_low = split(a)
    b_high, b_low = split(b)

    def one(x, y):
        return lax.dot_general(x, y, (dims, ((), ())), preferred_element_type=F32)

    return one(a_high, b_high) + (one(a_high, b_low) + one(a_low, b_high))


def row_of(x, i):
    return jnp.broadcast_to(x[i : i + 1, :], (GROUP, BASE))


def column_of(x, j):
    return jnp.broadcast_to(x[:, j : j + 1], (GROUP, BASE))


def factor_base(matrix):
    count = BASE // GROUP
    sub = lax.broadcasted_iota(jnp.int32, (GROUP, BASE), 0)
    lane = lax.broadcasted_iota(jnp.int32, (GROUP, BASE), 1)
    left = [matrix[m * GROUP : (m + 1) * GROUP, :] for m in range(count)]
    right = [(lane == sub + m * GROUP).astype(F32) for m in range(count)]
    spots = [jnp.where(right[m] > 0.0, left[m], 0.0) for m in range(count)]
    diagonal = jnp.sum(sum(spots), axis=0, keepdims=True)
    shrink = lax.rsqrt(diagonal)
    for m in range(count):
        tall = lax.rsqrt(jnp.sum(spots[m], axis=1, keepdims=True))
        left[m] = left[m] * tall * shrink
    upper, inverse = [], []
    for g in range(count):
        first = g * GROUP
        raw = [column_of(left[g], first + j) for j in range(GROUP)]
        s = {(i, j): row_of(raw[j], i) for i in range(GROUP) for j in range(i, GROUP)}
        rows = [row_of(left[g], i) for i in range(GROUP)]
        extra = [row_of(right[g], i) for i in range(GROUP)]
        scale, u = [None] * GROUP, {}
        for p in range(0, GROUP, 2):
            q = p + 1
            a, b = s[p, p], s[p, q]
            r = lax.rsqrt(a)
            d = lax.rsqrt(a * s[q, q] - b * b)
            both = d * r
            scale[p], scale[q] = r, a * both
            u[p, q] = b * r
            for j in range(q + 1, GROUP):
                u[p, j] = s[p, j] * r
                u[q, j] = (a * s[q, j] - b * s[p, j]) * both
            for j in range(q + 1, GROUP):
                for k in range(j, GROUP):
                    s[j, k] = (s[j, k] - u[p, j] * u[p, k]) - u[q, j] * u[q, k]
            for x in (rows, extra):
                x[p] = x[p] * r
                x[q] = (x[q] - u[p, q] * x[p]) * scale[q]
                for j in range(q + 1, GROUP):
                    x[j] = (x[j] - u[p, j] * x[p]) - u[q, j] * x[q]
        top, bottom = rows[0], extra[0]
        for i in range(1, GROUP):
            top = jnp.where(sub == i, rows[i], top)
            bottom = jnp.where(sub == i, extra[i], bottom)
        upper.append(jnp.where(lane >= sub + first, top, 0.0))
        inverse.append(bottom)
        if g + 1 == count:
            break
        m = g + 1
        left_sum, right_sum = left[m], right[m]
        columns = [column_of(left[m], first + i) for i in range(GROUP)]
        for i in range(GROUP):
            columns[i] = columns[i] * scale[i]
            for j in range(i + 1, GROUP):
                columns[j] = columns[j] - u[i, j] * columns[i]
            left_sum = left_sum - columns[i] * rows[i]
            right_sum = right_sum - columns[i] * extra[i]
        left[m], right[m] = left_sum, right_sum
        if g + 2 == count:
            continue
        back, back_extra = [None] * GROUP, [None] * GROUP
        for i in reversed(range(GROUP)):
            a, b = rows[i], extra[i]
            for k in range(i + 1, GROUP):
                a = a - u[i, k] * back[k]
                b = b - u[i, k] * back_extra[k]
            back[i], back_extra[i] = a * scale[i], b * scale[i]
        far_left = jnp.stack(left[g + 2 :])
        left_sum, right_sum = far_left, jnp.stack(right[g + 2 :])
        for i in range(GROUP):
            column = jnp.broadcast_to(far_left[:, :, first + i : first + i + 1], far_left.shape)
            left_sum = left_sum - column * back[i][None]
            right_sum = right_sum - column * back_extra[i][None]
        for m in range(g + 2, count):
            left[m] = left_sum[m - g - 2]
            right[m] = right_sum[m - g - 2]
    upper = jnp.concatenate(upper, axis=0) * (diagonal * shrink)
    return upper, jnp.concatenate(inverse, axis=0) * shrink


LEVELS = 32767.0
TINY = 1e-30


def fused_kernel(
    rows,
    cols,
    pivots_ref,
    targets_ref,
    own_ref,
    factor_ref,
    out_ref,
    work,
    u_ref,
    p_ref,
    slabs,
    outgoing,
    out_scale,
    received,
    in_scale,
    row_send,
    row_recv,
    send_sem,
    recv_sem,
):
    block = own_ref.shape[0]
    width = own_ref.shape[1]
    blocks = width // block
    own_first = STEPS * block
    row = lax.axis_index("row")
    col = lax.axis_index("col")
    core = lax.rem(row, 2)
    partner = row + 1 - 2 * core
    pivot_count = pivots_ref[col]
    own_columns = pl.ds(pl.multiple_of(row * block, block), block)

    barrier = pltpu.get_barrier_semaphore()
    for step in range(1, rows):
        pl.semaphore_signal(
            barrier, inc=1, device_id={"row": lax.rem(row + step, rows)}, device_id_type=MESH
        )
    for step in range(1, cols):
        pl.semaphore_signal(
            barrier, inc=1, device_id={"col": lax.rem(col + step, cols)}, device_id_type=MESH
        )
    pl.semaphore_wait(barrier, rows + cols - 2)

    pieces = [(0, 0, block), (0, block, width - block)]
    pieces += [(t, t * block, width - t * block) for t in range(1, STEPS)]

    def piece_copy(piece, source, target, slot):
        t, first, size = pieces[piece]
        columns = pl.ds(first, size)
        return pltpu.make_async_remote_copy(
            src_ref=source.at[:, columns] if source is own_ref else source.at[t, :, columns],
            dst_ref=slabs.at[t, :, columns],
            send_sem=row_send.at[piece, slot],
            recv_sem=row_recv.at[piece],
            device_id={"row": target},
            device_id_type=MESH,
        )

    def owner_copies(piece):
        slot = 0
        t = pieces[piece][0]
        copies = []
        for y in range(rows // 2):
            target = 2 * y + t % 2
            if target != t:
                copies.append(piece_copy(piece, own_ref, target, slot))
                slot += 1
        copies.append(piece_copy(piece, own_ref, t + 1 - 2 * (t % 2), slot))
        return copies

    def send_piece(piece):
        @pl.when(row == pieces[piece][0])
        def _():
            for copy in owner_copies(piece):
                copy.start()

    def arrive(piece):
        t, first, size = pieces[piece]

        @pl.when(row != t)
        def _():
            piece_copy(piece, slabs, partner, 0).wait_recv()

            @pl.when(core == t % 2)
            def _():
                piece_copy(piece, slabs, partner, 0).start()

            work[pl.ds(t * block, block), pl.ds(first, size)] = slabs[
                t, :, pl.ds(first, size)
            ].astype(F32)

        @pl.when(row == t)
        def _():
            work[pl.ds(t * block, block), pl.ds(first, size)] = own_ref[
                :, pl.ds(first, size)
            ].astype(F32)

    def chunk_of(first):
        return width - first if width <= 1024 else block

    def chunks(body, first):
        size = chunk_of(first)
        if width <= 1024:
            body(first)
        else:
            pl.loop(0, (width - first) // size)(
                lambda c: body(pl.multiple_of(first + c * size, size))
            )

    def part_of(part, diagonal):
        first = BASE if diagonal and part else 0
        return pl.ds(first, block - first), pl.ds(part * BASE, BASE)

    def block_copies(j, upper, diagonal):
        pairs = [
            (outgoing.at[j, *place], received.at[col, *place], send_sem, recv_sem, part)
            for part, place in enumerate((part_of(0, diagonal), part_of(1, diagonal)))
        ]
        pairs.append((out_scale.at[j], in_scale.at[col], send_sem, recv_sem, 2))
        return [
            pltpu.make_async_remote_copy(
                src_ref=source,
                dst_ref=sink,
                send_sem=sends.at[j, upper, part],
                recv_sem=recvs.at[col, part],
                device_id={"col": j + upper * blocks},
                device_id_type=MESH,
            )
            for source, sink, sends, recvs, part in pairs
        ]

    def send_block(j):
        x = work[own_first:, j * block : (j + 1) * block]
        top = jnp.maximum(jnp.max(jnp.abs(x), axis=0, keepdims=True), TINY)
        outgoing[j] = jnp.floor(x * (LEVELS / top) + 0.5).astype(jnp.int32).astype(jnp.int16)
        out_scale[j] = jnp.broadcast_to(top * (1.0 / LEVELS), (GROUP, block))
        for upper in (1, 0):
            for diagonal in (False, True):

                @pl.when((col != j + upper * blocks) & ((row == j) == diagonal))
                def _():
                    for copy in block_copies(j, upper, diagonal):
                        copy.start()

            @pl.when(col == j + upper * blocks)
            def _():
                received[col] = outgoing[j]
                in_scale[col] = out_scale[j]

    def direct(source, t, height, first, size, target, index, slot):
        place = (pl.ds(0, height), pl.ds(first, size))
        return pltpu.make_async_remote_copy(
            src_ref=source.at[place],
            dst_ref=slabs.at[t, *place],
            send_sem=row_send.at[index, slot],
            recv_sem=row_recv.at[index],
            device_id={"row": target},
            device_id_type=MESH,
        )

    shares = [(0, BASE, 0, BASE), (0, block, BASE, block - BASE), (0, block, block, block)]
    shares += [(1, block, block, block)]

    def share(index, target):
        return direct(own_ref, *shares[index], target, index, target - 2)

    def take(index):
        t, height, first, size = shares[index]
        work[pl.ds(t * block, height), pl.ds(first, size)] = slabs[
            t, :height, pl.ds(first, size)
        ].astype(F32)

    def flip(source, t, j):
        x = source[:, t * block : (t + 1) * block].astype(F32)
        work[t * block : (t + 1) * block, j * block : (j + 1) * block] = x.T

    def flips(source, j):
        for t in range(2):
            flip(source, t, j)

    def partner_copy(r):
        if r == 0:
            return direct(own_ref, 0, block, 0, width, 1, 4, 0)
        size = width if r == 2 else 2 * block
        return direct(own_ref, 2, block, 0, size, 5 - r, 4, 0)

    def pair_start():
        @pl.when(row == 0)
        def _():
            for target in (2, 3):
                share(0, target).start()
            partner_copy(0).start()
            for index in (1, 2):
                for target in (2, 3):
                    share(index, target).start()

        for r in (2, 3):

            @pl.when(row == r)
            def _():
                partner_copy(r).start()

        work[own_first:, :] = own_ref[...].astype(F32)
        work[:own_first, :block] = jnp.zeros((own_first, block), F32)
        work[2 * block : own_first, : 2 * block] = jnp.zeros((block, 2 * block), F32)

        @pl.when(row == 0)
        def _():
            work[:block, :] = own_ref[...].astype(F32)

        @pl.when(row == 1)
        def _():
            partner_copy(0).wait_recv()
            for target in (2, 3):
                share(3, target).start()
            work[:block, :] = slabs[0].astype(F32)
            work[block : 2 * block, :] = own_ref[...].astype(F32)

        for r in (2, 3):

            @pl.when(row == r)
            def _():
                flips(own_ref, r)
                if r == 2:
                    work[2 * block : own_first, :] = own_ref[...].astype(F32)
                share(0, r).wait_recv()
                take(0)

    def pair_middle():
        for r in (2, 3):

            @pl.when(row == r)
            def _():
                partner_copy(5 - r).wait_recv()
                flips(slabs.at[2], 5 - r)
                if r == 3:
                    work[2 * block : own_first, :] = slabs[2].astype(F32)
                for index in (1, 2):
                    share(index, r).wait_recv()
                    take(index)

    def pair_late():
        for r in (2, 3):

            @pl.when(row == r)
            def _():
                share(3, r).wait_recv()
                take(3)

    def pair_finish():
        @pl.when(row == 0)
        def _():
            for target in (2, 3):
                for index in (0, 1, 2):
                    share(index, target).wait_send()
            partner_copy(0).wait_send()

        @pl.when(row == 1)
        def _():
            for target in (2, 3):
                share(3, target).wait_send()

        for r in (2, 3):

            @pl.when(row == r)
            def _():
                partner_copy(r).wait_send()

    def slab_start():
        send_piece(0)
        send_piece(1)
        work[own_first:, :] = own_ref[...].astype(F32)
        for t in range(1, STEPS):
            work[t * block : (t + 1) * block, : t * block] = jnp.zeros((block, t * block), F32)
        arrive(0)
        for piece in range(2, len(pieces)):
            send_piece(piece)

    def slab_middle():
        arrive(1)

    def slab_late():
        for piece in range(2, len(pieces)):
            arrive(piece)

    def slab_finish():
        for piece in range(len(pieces)):
            t = pieces[piece][0]

            @pl.when(row == t)
            def _():
                for copy in owner_copies(piece):
                    copy.wait_send()

            @pl.when((row != t) & (core == t % 2))
            def _():
                piece_copy(piece, slabs, partner, 0).wait_send()

    if rows == 4 and blocks == 4:
        start, middle, late, finish = pair_start, pair_middle, pair_late, pair_finish
    else:
        start, middle, late, finish = slab_start, slab_middle, slab_late, slab_finish
    start()
    tri_row = lax.broadcasted_iota(jnp.int32, (block, block), 0)
    tri_column = lax.broadcasted_iota(jnp.int32, (block, block), 1)
    factor_ref[:, block:] = jnp.zeros((block, (STEPS - 1) * block), F32)

    def step(t):
        active = t < pivot_count
        top = pl.ds(t * block, BASE)
        low = pl.ds(t * block + BASE, BASE)
        after = (t + 1) * block
        upper, inverse = factor_base(work[top, top])
        if t == 0:
            middle()

        cross = dot3(inverse, work[top, low], ((1,), (0,)))
        low_upper, low_inverse = factor_base(work[low, low] - dot3(cross, cross, ((0,), (0,))))

        def solve(c):
            columns = pl.ds(c, chunk_of(after))
            solved = dot3(inverse, work[top, columns], ((1,), (0,)))
            u_ref[:BASE, columns] = solved
            work[low, columns] -= dot3(cross, solved, ((0,), (0,)))

        def solve_low(c):
            columns = pl.ds(c, chunk_of(after))
            u_ref[BASE:, columns] = dot3(low_inverse, work[low, columns], ((1,), (0,)))

        chunks(solve, after)
        chunks(solve_low, after)
        u_ref[:BASE, top] = upper
        u_ref[:BASE, low] = cross
        u_ref[BASE:, top] = jnp.zeros((BASE, BASE), F32)
        u_ref[BASE:, low] = low_upper

        def round_panel(c):
            columns = pl.ds(c, chunk_of(after))
            p_ref[:, columns] = jnp.where(active, u_ref[:, columns], 0.0).astype(BF16)

        chunks(round_panel, after)
        if t == 0:
            late()
        keep = active & ((row > t) | (tri_row >= tri_column))
        factor_ref[:, t * block : after] = jnp.where(
            keep, -u_ref[:, own_columns].T, 0.0
        )

        def outer(left, columns):
            dims = (((0,), (0,)), ((), ()))
            return lax.dot_general(left, p_ref[:, columns], dims, preferred_element_type=F32)

        def trail(c):
            columns = pl.ds(c, chunk_of(after))
            if after < own_first:
                work[after:own_first, columns] -= outer(p_ref[:, after:own_first], columns)
            work[pl.ds(own_first, block), columns] -= outer(p_ref[:, own_columns], columns)

        @pl.when(row == t)
        def _():
            p_ref[:, own_columns] = jnp.zeros((block, block), BF16)

        chunks(trail, after)
        for j in range(1, blocks):
            level = jnp.minimum(row, min(j, STEPS))

            @pl.when(level == t + 1)
            def _():
                send_block(j)

    for t in range(STEPS):

        @pl.when(row >= t)
        def _():
            step(t)

    out_ref[...] = jnp.zeros_like(out_ref)
    mine = lax.rem(col, blocks)

    def collect(diagonal):
        @pl.loop(0, cols)
        def _(source):
            places = [part_of(0, diagonal), part_of(1, diagonal)]

            @pl.when(source != col)
            def _():
                sinks = [received.at[source, *place] for place in places]
                for part, sink in enumerate([*sinks, in_scale.at[source]]):
                    pltpu.make_async_remote_copy(
                        src_ref=sink,
                        dst_ref=sink,
                        send_sem=recv_sem.at[source, part],
                        recv_sem=recv_sem.at[source, part],
                        device_id={"col": source},
                        device_id_type=MESH,
                    ).wait_recv()

            used = (pivots_ref[source] <= jnp.minimum(row, mine)) & (
                targets_ref[mine, source] == col
            )
            high = targets_ref[row, source] >= blocks
            for place in places:
                values = received[source, *place].astype(jnp.int32).astype(F32)
                scale = in_scale[source, 0:1, place[1]]
                out_ref[0, *place] += values * jnp.where(used & ~high, scale, 0.0)
                out_ref[1, *place] += values * jnp.where(used & high, scale, 0.0)

        if diagonal:
            for half in range(2):
                out_ref[half, :BASE, BASE:] = out_ref[half, BASE:, :BASE].T

    for diagonal in (False, True):

        @pl.when((row >= 1) & (mine >= 1) & ((row == mine) == diagonal))
        def _():
            collect(diagonal)

    finish()

    for j in range(1, blocks):
        for upper in (1, 0):
            for diagonal in (False, True):

                @pl.when((row >= 1) & (col != j + upper * blocks) & ((row == j) == diagonal))
                def _():
                    for copy in block_copies(j, upper, diagonal):
                        copy.wait_send()


def shards(rows, cols, fronts, pivots, targets, ancestor):
    block, width = fronts.shape[1:]
    blocks = width // block
    vmem = pl.BlockSpec(memory_space=pltpu.VMEM)
    smem = pl.BlockSpec(memory_space=pltpu.SMEM)
    dma = pltpu.SemaphoreType.DMA
    negated, added = pl.pallas_call(
        functools.partial(fused_kernel, rows, cols),
        out_shape=(
            jax.ShapeDtypeStruct((block, STEPS * block), F32),
            jax.ShapeDtypeStruct(ancestor.shape, F32),
        ),
        in_specs=[smem, smem, vmem],
        out_specs=(vmem, vmem),
        scratch_shapes=[
            pltpu.VMEM(((STEPS + 1) * block, width), F32),
            pltpu.VMEM((block, width), F32),
            pltpu.VMEM((block, width), BF16),
            pltpu.VMEM((STEPS, block, width), BF16),
            pltpu.VMEM((blocks, block, block), jnp.int16),
            pltpu.VMEM((blocks, GROUP, block), F32),
            pltpu.VMEM((cols, block, block), jnp.int16),
            pltpu.VMEM((cols, GROUP, block), F32),
            dma((STEPS + 2, rows // 2)),
            dma((STEPS + 2,)),
            dma((blocks, 2, 3)),
            dma((cols, 3)),
        ],
        compiler_params=pltpu.CompilerParams(
            collective_id=0, has_side_effects=True, vmem_limit_bytes=56 * 1024 * 1024
        ),
    )(pivots, targets.T, fronts[0])
    return (-negated[None], ancestor.astype(F32) + added)


def solution(mesh):
    in_specs = (P("col", "row", None), P(), P(), P(None, "row", "col"))
    out_specs = (P("col", "row", None), P(None, "row", "col"))
    body = functools.partial(shards, mesh.shape["row"], mesh.shape["col"])
    return jax.shard_map(body, mesh=mesh, in_specs=in_specs, out_specs=out_specs, check_vma=False)
```
